32 devices in a mesh: shot: 2 (over y), gx: 16 (over z, x, core).
Axes of the slice: x: 2, y: 2, z: 4, core: 2. Of those that a mesh axis runs over, the one named last changes fastest.
Arguments:
- wave_now: float32 [4, 256, 16, 256], P('shot', 'gx'), parts along dimension 0, may hold values from -18 to 18
- wave_prev: float32 [4, 256, 16, 256], P('shot', 'gx'), parts along dimension 0, may hold values from -18 to 18
- courant: float32 [256, 32, 256], P('gx', 'shot'), parts along dimension 1, may hold values from 0.09 to 0.17
- epsilon: float32 [256, 32, 256], P('gx', 'shot'), parts along dimension 1, may hold values from 0.15 to 0.3
- tilt: float32 [256, 32, 256], P('gx', 'shot'), parts along dimension 1, may hold values from -0.5 to 0.5
- trace_index: int32 [256, 512], P('gx', 'shot'), parts along dimension 1, may hold values from 0 to 2047
- traces: float32 [32, 2048], P('shot'), parts along dimension 0, may hold values from -6 to 6
- lag_list: int32 [33], replicated, may hold values from 0 to 32, each once
Outputs:
- image_out: bfloat16 [66, 256, 16, 256], P('shot', 'gx'), parts along dimension 0
- wave_out: float32 [4, 256, 16, 256], P('shot', 'gx'), parts along dimension 0
The draws below stay inside these ranges and needn't reach their ends.
There are 2 independent parts, one for each index of `shot`. The reference program is written for one: setup_inputs(seed, part) draws one part's arguments, and reference() takes and returns one part's arrays. A program takes and returns all parts, laid end to end along the dimension named above; an argument that names none is the same for every part. Nothing has to cross between parts.
Inputs may be any that keep to these rules, and one draw needn't show every extreme that they name: Each of 0 to 32 once; entry k selects offset lag_list[k] - 16.
All inputs are finite; a program needn't handle non-finite values.
Results may differ from the reference program's by a relative error of at most 0.0058.
Values may be sent and summed in bfloat16 or wider, within the bound.
A program may use at most 128 MiB of HBM per device.

```python
import math
import jax
import jax.numpy as jnp
from jax import lax

NZ = 16
NY = 256
SUB = 4
SNAPS = 4
LAGS = 33
NTRACE = 2048
HALF = 16
STEPS = 16
NX = 256


def field_scales():
    return jnp.array([3.0, 1.0 / 3.0], jnp.float32).reshape(2, 1, 1, 1)


def draw_wave_now(key, part):
    key = jax.random.fold_in(key, 11)
    base = jnp.clip(jax.random.normal(key, (2, NX, NZ, NY), jnp.float32), -6.0, 6.0)
    return base * field_scales()


def draw_wave_prev(key, part):
    key = jax.random.fold_in(key, 12)
    base = jnp.clip(jax.random.normal(key, (2, NX, NZ, NY), jnp.float32), -6.0, 6.0)
    return base * field_scales()


def with_ends(result, key, smallest, top_value):
    spot = [jax.random.randint(jax.random.fold_in(key, axis), (), 0, length) for axis, length in enumerate(result.shape)]
    main_axis = result.shape.index(max(result.shape))
    neighbour = spot[:main_axis] + [(spot[main_axis] + 1) % result.shape[main_axis]] + spot[main_axis + 1:]
    return result.at[tuple(spot)].set(smallest).at[tuple(neighbour)].set(top_value)


def block_levels(rng, dims, cuts, low, high):
    def one(position, parts):
        heights = jax.random.uniform(jax.random.fold_in(jax.random.fold_in(rng, 6), position), (parts,), jnp.float32, low / len(cuts), high / len(cuts))
        return jnp.repeat(jnp.exp(heights), dims[position] // parts).reshape((-1,) + (1,) * (len(dims) - position - 1))

    loudness = one(*cuts[0])
    for cut in cuts[1:]:
        loudness = loudness * one(*cut)
    return loudness


def bell_draw(stream_key, dims, spread, reach, dtype=jnp.bfloat16):
    result = spread * jax.random.normal(stream_key, dims, jnp.float32)
    return jnp.clip(result, min=-reach, max=reach).astype(dtype)


def setup_inputs(seed: int = 0, part: int = 0) -> dict:
    key_list = jax.random.split(jax.random.key(seed), 9)
    own_keys = jax.random.split(jax.random.fold_in(key_list[8], part), 9)
    wave_now = draw_wave_now(jax.random.fold_in(jax.random.fold_in(key_list[8], part), 71), part)
    wave_prev = draw_wave_prev(jax.random.fold_in(jax.random.fold_in(key_list[8], part), 71), part)
    courant = jnp.clip(jnp.exp(math.log(0.17) - 0.6359887 * jax.random.uniform(own_keys[2], (NX, NZ, NY), jnp.float32) ** block_levels(own_keys[2], (NX, NZ, NY), ((0, 16),), -0.2, 0.2)), 0.09, 0.17)
    epsilon = jnp.clip(0.15 + 0.15 * jax.random.uniform(own_keys[3], (NX, NZ, NY), jnp.float32) ** block_levels(own_keys[3], (NX, NZ, NY), ((0, 16),), -0.2, 0.2), 0.15, 0.3)
    tilt = jnp.clip(jax.random.uniform(own_keys[4], (NX, NZ, NY), jnp.float32, -0.5, 0.5) * block_levels(own_keys[4], (NX, NZ, NY), ((0, 16),), -0.4, 0.0), -0.5, 0.5)
    trace_index = with_ends(jax.random.randint(own_keys[5], (NX, NY), 0, NTRACE), jax.random.fold_in(own_keys[5], 1), 0, NTRACE - 1).astype(jnp.int32)
    traces = bell_draw(own_keys[6], (STEPS, NTRACE), 1.0, 6.0, jnp.float32)
    lag_list = jax.random.permutation(key_list[7], LAGS).astype(jnp.int32)
    return {"wave_now": wave_now, "wave_prev": wave_prev, "courant": courant, "epsilon": epsilon, "tilt": tilt, "trace_index": trace_index, "traces": traces, "lag_list": lag_list}


CENTER = -2.5
NEAR = 4.0 / 3.0
FAR = -1.0 / 12.0


def coefficients(epsilon, tilt):
    cosine_tilt = jnp.cos(tilt)
    sine_tilt = jnp.sin(tilt)
    stretch = 1.0 + 2.0 * epsilon
    coef_a = stretch * cosine_tilt * cosine_tilt + sine_tilt * sine_tilt
    coef_b = stretch * sine_tilt * sine_tilt + cosine_tilt * cosine_tilt
    coef_c = 2.0 * epsilon * jnp.sin(2.0 * tilt)
    return coef_a, coef_b, coef_c


def operator(extended, coef_a, coef_b, coef_c):
    length_out = extended.shape[1] - 4
    depth_cells = extended.shape[2]
    cross_cells = extended.shape[3]
    padded = jnp.pad(extended, ((0, 0), (0, 0), (2, 2), (2, 2)))

    def shifted(move_x, move_z, move_y):
        return padded[:, 2 + move_x:2 + move_x + length_out, 2 + move_z:2 + move_z + depth_cells, 2 + move_y:2 + move_y + cross_cells]

    middle = shifted(0, 0, 0)
    second_x = CENTER * middle + NEAR * (shifted(1, 0, 0) + shifted(-1, 0, 0)) + FAR * (shifted(2, 0, 0) + shifted(-2, 0, 0))
    second_z = CENTER * middle + NEAR * (shifted(0, 1, 0) + shifted(0, -1, 0)) + FAR * (shifted(0, 2, 0) + shifted(0, -2, 0))
    second_y = CENTER * middle + NEAR * (shifted(0, 0, 1) + shifted(0, 0, -1)) + FAR * (shifted(0, 0, 2) + shifted(0, 0, -2))
    mixed = 0.25 * (shifted(1, 1, 0) - shifted(1, -1, 0) - shifted(-1, 1, 0) + shifted(-1, -1, 0))
    return coef_a * second_x + coef_b * second_z + second_y + coef_c * mixed


def reference(wave_now, wave_prev, courant, epsilon, tilt, trace_index, traces, lag_list):
    coef_a, coef_b, coef_c = coefficients(epsilon, tilt)
    inject = traces[:, trace_index]
    current = wave_now
    previous = wave_prev
    snapshots = []
    for block_index in range(SNAPS):
        snapshots.append(current.astype(jnp.bfloat16))
        for substep in range(SUB):
            beside_all = jnp.pad(current, ((0, 0), (2, 2), (0, 0), (0, 0)))
            advanced = 2.0 * current - previous + courant * operator(beside_all, coef_a, coef_b, coef_c)
            advanced = advanced.at[1, :, 0, :].add(inject[block_index * SUB + substep])
            previous, current = current, advanced
    padded = jnp.pad(jnp.stack(snapshots), ((0, 0), (0, 0), (HALF, HALF), (0, 0), (0, 0)))

    def one_offset(entry):
        offset = entry.astype(jnp.int32) - HALF

        def accumulate(image_sum, snapshot):
            source = lax.dynamic_slice_in_dim(snapshot[0], (HALF - offset).astype(jnp.int32), NX, 0)
            receiver = lax.dynamic_slice_in_dim(snapshot[1], (HALF + offset).astype(jnp.int32), NX, 0)
            return image_sum + source.astype(jnp.float32) * receiver.astype(jnp.float32), None

        image_sum, _ = lax.scan(accumulate, jnp.zeros((NX, NZ, NY), jnp.float32), padded)
        return image_sum.astype(jnp.bfloat16)

    image_out = lax.map(one_offset, lag_list)
    return (image_out, current)
```

```python
import functools

import jax
import jax.numpy as jnp
from jax import lax
from jax.experimental import pallas as pl
from jax.experimental.pallas import tpu as pltpu
from jax.sharding import PartitionSpec as P

SUB = 4
SNAPS = 4
STEPS = 16
LAGS = 33
HALF = 16
MESH = pl.DeviceIdType.MESH
LIMIT = 48 * 1024 * 1024


def prep_kernel(courant, epsilon, tilt, index, traces, coefs, inject):
    def layer(x, carry):
        c = courant[x]
        e2 = 2.0 * epsilon[x]
        s = jnp.sin(tilt[x])
        k = jnp.cos(tilt[x])
        a = c * (1.0 + e2 * k * k)
        b = c * (1.0 + e2 * s * s)
        coefs[0, x] = 2.0 - 2.5 * (a + b + c)
        coefs[1, x] = (4.0 / 3.0) * a
        coefs[2, x] = (4.0 / 3.0) * b
        coefs[3, x] = (4.0 / 3.0) * c
        coefs[4, x] = 0.5 * c * e2 * s * k
        return carry

    lax.fori_loop(0, courant.shape[0], layer, 0)

    rows, columns = index.shape
    pieces = [(r, y) for r in range(0, rows, 8) for y in range(0, columns, 128)]
    low = []
    high = []
    for r, y in pieces:
        i = index[r : r + 8, y : y + 128]
        low.append(i & 127)
        high.append(i >> 7)

    def at_time(t, carry):
        found = [jnp.zeros((8, 128), jnp.float32) for _ in pieces]
        for h in range(traces.shape[1]):
            row = jnp.broadcast_to(traces[t, h : h + 1], (8, 128))
            for p in range(len(pieces)):
                value = jnp.take_along_axis(row, low[p], axis=1, mode="promise_in_bounds")
                found[p] = jnp.where(high[p] == h, value, found[p])
        for (r, y), value in zip(pieces, found):
            for i in range(8):
                inject[t, r + i, :, y : y + 128] = value[i : i + 1]
        return carry

    lax.fori_loop(0, traces.shape[0], at_time, 0)


def wave_kernel(
    count,
    wave_now, wave_prev, coefs, inject,
    wave_out, snaps,
    even, odd, send, halo, own, zero,
    local_sem, send_sem, recv_sem, snap_send, snap_recv, snap_local, zero_sem,
):
    width = wave_now.shape[1]
    shot = lax.axis_index("shot")
    me = lax.axis_index("gx")
    has_left = me > 0
    has_right = me < count - 1
    sides = ((0, has_left, me - 1), (1, has_right, me + 1))

    barrier = pltpu.get_barrier_semaphore()
    for _, there, other in sides:
        @pl.when(there)
        def _():
            pl.semaphore_signal(barrier, inc=1, device_id=(shot, other), device_id_type=MESH)

    load_now = pltpu.make_async_copy(wave_now, even.at[:, pl.ds(2, width)], local_sem.at[0])
    load_prev = pltpu.make_async_copy(wave_prev, odd.at[:, pl.ds(2, width)], local_sem.at[1])
    load_now.start()
    load_prev.start()

    for side, there, _ in sides:
        @pl.when(jnp.logical_not(there))
        def _():
            zero[...] = jnp.zeros(zero.shape, zero.dtype)
            for ref in (even, odd):
                ref[:, pl.ds(side * (width + 2), 2)] = jnp.zeros((2, 2) + ref.shape[2:], ref.dtype)

    def edge_copies():
        found = []
        for side, there, _ in sides:
            for b in range(SNAPS):
                for f in range(2):
                    found.append((there, pltpu.make_async_copy(
                        zero, snaps.at[b, f, pl.ds(side * 2 * width, width)],
                        zero_sem.at[side, b, f])))
        return found

    for there, copy in edge_copies():
        @pl.when(jnp.logical_not(there))
        def _():
            copy.start()

    pl.semaphore_wait(barrier, has_left.astype(jnp.int32) + has_right.astype(jnp.int32))

    def halo_copy(t, side, other):
        return pltpu.make_async_remote_copy(
            src_ref=send.at[t, side],
            dst_ref=halo.at[t, 1 - side],
            send_sem=send_sem.at[t, side],
            recv_sem=recv_sem.at[t, 1 - side],
            device_id=(shot, other),
            device_id_type=MESH,
        )

    def halo_arrival(t, side, other):
        return pltpu.make_async_remote_copy(
            src_ref=send.at[t, side],
            dst_ref=halo.at[t, side],
            send_sem=send_sem.at[t, side],
            recv_sem=recv_sem.at[t, side],
            device_id=(shot, other),
            device_id_type=MESH,
        )

    def snap_copy(b, side, other, place):
        return pltpu.make_async_remote_copy(
            src_ref=own.at[b],
            dst_ref=snaps.at[b, :, pl.ds(place * 2 * width, width)],
            send_sem=snap_send.at[b, side],
            recv_sem=snap_recv.at[b, place],
            device_id=(shot, other),
            device_id_type=MESH,
        )

    def own_copy(b):
        return pltpu.make_async_copy(own.at[b], snaps.at[b, :, pl.ds(width, width)], snap_local.at[b])

    def send_edges(t, ref):
        for side, there, other in sides:
            @pl.when(there)
            def _():
                send[t, side] = ref[:, pl.ds(2 + side * (width - 2), 2)].astype(jnp.bfloat16)
                halo_copy(t, side, other).start()

    depth, cross = wave_now.shape[2:]
    z = lax.broadcasted_iota(jnp.int32, (depth, cross), 0)
    y = lax.broadcasted_iota(jnp.int32, (depth, cross), 1)

    def shift_z(u, move):
        moved = pltpu.roll(u, (-move) % depth, 0)
        inside = (z < depth - move) if move > 0 else (z >= -move)
        return jnp.where(inside, moved, 0.0)

    def shift_y(u, move):
        moved = pltpu.roll(u, (-move) % cross, 1)
        inside = (y < cross - move) if move > 0 else (y >= -move)
        return jnp.where(inside, moved, 0.0)

    def advance(now, prev, t, x):
        centre, cx, cz, cy, cm = (coefs[i, x] for i in range(5))
        row = jnp.broadcast_to(inject[t, x], (depth, cross))
        for f in range(2):
            u = now[f, x + 2]
            before = now[f, x + 1]
            after = now[f, x + 3]
            total = centre * u - prev[f, x + 2]
            total += cx * ((before + after) - (now[f, x] + now[f, x + 4]) * 0.0625)
            far_z = shift_z(u, 2) + shift_z(u, -2)
            total += cz * ((shift_z(u, 1) + shift_z(u, -1)) - far_z * 0.0625)
            far_y = shift_y(u, 2) + shift_y(u, -2)
            total += cy * ((shift_y(u, 1) + shift_y(u, -1)) - far_y * 0.0625)
            across = after - before
            total += cm * (shift_z(across, 1) - shift_z(across, -1))
            if f == 1:
                total += jnp.where(z == 0, row, 0.0)
            prev[f, x + 2] = total

    load_now.wait()
    send_edges(0, even)
    load_prev.wait()

    def block(b, carry):
        for j in range(SUB):
            now, prev = (even, odd) if j % 2 == 0 else (odd, even)
            t = b * SUB + j
            if j == 0:
                own[b] = now[:, pl.ds(2, width)].astype(jnp.bfloat16)
                own_copy(b).start()
                for side, there, other in sides:
                    @pl.when(there)
                    def _():
                        snap_copy(b, side, other, 1 - side).start()

            def inner(x, c):
                advance(now, prev, t, x)
                return c

            lax.fori_loop(2, width - 2, inner, 0)
            for side, there, other in sides:
                @pl.when(there)
                def _():
                    halo_arrival(t, side, other).wait_recv()
                    now[:, pl.ds(side * (width + 2), 2)] = halo[t, side].astype(jnp.float32)

                def edge(i, c):
                    advance(now, prev, t, side * (width - 2) + i)
                    return c

                lax.fori_loop(0, 2, edge, 0)

            if j < SUB - 1:
                send_edges(t + 1, prev)
            else:
                @pl.when(b < SNAPS - 1)
                def _():
                    send_edges(t + 1, prev)
        return carry

    lax.fori_loop(0, SNAPS, block, 0)

    store = pltpu.make_async_copy(even.at[:, pl.ds(2, width)], wave_out, local_sem.at[0])
    store.start()
    for side, there, other in sides:
        @pl.when(there)
        def _():
            def drain(t, c):
                halo_copy(t, side, other).wait_send()
                return c

            lax.fori_loop(0, STEPS, drain, 0)
            for b in range(SNAPS):
                snap_copy(b, side, other, 1 - side).wait_send()
                snap_copy(b, side, other, side).wait_recv()
    for there, copy in edge_copies():
        @pl.when(jnp.logical_not(there))
        def _():
            copy.wait()
    for b in range(SNAPS):
        own_copy(b).wait()
    store.wait()


def correlate_kernel(lags, snaps, image):
    h = lags[pl.program_id(0)] - HALF
    width = image.shape[1]
    for x in range(width):
        terms = [snaps[b, 0, HALF - h + x] * snaps[b, 1, HALF + h + x] for b in range(SNAPS)]
        image[0, x] = (terms[0] + terms[1]) + (terms[2] + terms[3])


def body(count, wave_now, wave_prev, courant, epsilon, tilt, trace_index, traces, lag_list):
    _, width, depth, cross = wave_now.shape
    vmem = pl.BlockSpec(memory_space=pltpu.VMEM)
    whole = pl.BlockSpec(memory_space=pl.ANY)
    coefs, inject = pl.pallas_call(
        prep_kernel,
        out_shape=(
            jax.ShapeDtypeStruct((5, width, depth, cross), jnp.float32),
            jax.ShapeDtypeStruct((STEPS, width, 1, cross), jnp.float32),
        ),
        in_specs=[vmem] * 5,
        out_specs=(vmem, vmem),
        compiler_params=pltpu.CompilerParams(vmem_limit_bytes=LIMIT),
    )(courant, epsilon, tilt, trace_index, traces.reshape(STEPS, -1, 128))

    state = pltpu.VMEM((2, width + 4, depth, cross), jnp.float32)
    edges = pltpu.VMEM((STEPS, 2, 2, 2, depth, cross), jnp.bfloat16)
    dma = pltpu.SemaphoreType.DMA
    wave_out, snaps = pl.pallas_call(
        functools.partial(wave_kernel, count),
        out_shape=(
            jax.ShapeDtypeStruct(wave_now.shape, jnp.float32),
            jax.ShapeDtypeStruct((SNAPS, 2, 3 * width, depth, cross), jnp.bfloat16),
        ),
        in_specs=[whole, whole, vmem, vmem],
        out_specs=(whole, whole),
        scratch_shapes=[
            state, state, edges, edges,
            pltpu.VMEM((SNAPS, 2, width, depth, cross), jnp.bfloat16),
            pltpu.VMEM((width, depth, cross), jnp.bfloat16),
            dma((2,)),
            dma((STEPS, 2)),
            dma((STEPS, 2)),
            dma((SNAPS, 2)),
            dma((SNAPS, 2)),
            dma((SNAPS,)),
            dma((2, SNAPS, 2)),
        ],
        compiler_params=pltpu.CompilerParams(
            collective_id=0, has_side_effects=True, vmem_limit_bytes=LIMIT
        ),
    )(wave_now, wave_prev, coefs, inject)

    image_out = pl.pallas_call(
        correlate_kernel,
        out_shape=jax.ShapeDtypeStruct((LAGS, width, depth, cross), jnp.bfloat16),
        grid_spec=pltpu.PrefetchScalarGridSpec(
            num_scalar_prefetch=1,
            grid=(LAGS,),
            in_specs=[vmem],
            out_specs=pl.BlockSpec((1, width, depth, cross), lambda k, lags: (k, 0, 0, 0)),
        ),
        compiler_params=pltpu.CompilerParams(vmem_limit_bytes=LIMIT),
    )(lag_list, snaps)
    return (image_out, wave_out)


def solution(mesh):
    placed = (
        P("shot", "gx", None, None),
        P("shot", "gx", None, None),
        P("gx", "shot", None),
        P("gx", "shot", None),
        P("gx", "shot", None),
        P("gx", "shot"),
        P("shot", None),
        P(),
    )
    return jax.shard_map(
        functools.partial(body, mesh.shape["gx"]),
        mesh=mesh,
        in_specs=placed,
        out_specs=(P("shot", "gx", None, None), P("shot", "gx", None, None)),
        check_vma=False,
    )
```

```python
import functools

import jax
import jax.numpy as jnp
from jax import lax
from jax.experimental import pallas as pl
from jax.experimental.pallas import tpu as pltpu
from jax.sharding import PartitionSpec as P

SNAPS = 4
STEPS = 16
LAGS = 33
HALF = 16
GROUP = 11
PAIRS = STEPS // 2
DEEP = 4
MESH = pl.DeviceIdType.MESH
LIMIT = 48 * 1024 * 1024


def prep_kernel(courant, epsilon, tilt, index, traces, coefs, inject):
    def layer(x, carry):
        c = courant[x]
        e2 = 2.0 * epsilon[x]
        s = jnp.sin(tilt[x])
        k = jnp.cos(tilt[x])
        a = c * (1.0 + e2 * k * k)
        b = c * (1.0 + e2 * s * s)
        coefs[0, x] = 2.0 - 2.5 * (a + b + c)
        coefs[1, x] = (4.0 / 3.0) * a
        coefs[2, x] = (4.0 / 3.0) * b
        coefs[3, x] = (4.0 / 3.0) * c
        coefs[4, x] = 0.5 * c * e2 * s * k
        return carry

    lax.fori_loop(0, courant.shape[0], layer, 0)

    rows, columns = index.shape
    pieces = [(r, y) for r in range(0, rows, 8) for y in range(0, columns, 128)]
    low = []
    high = []
    for r, y in pieces:
        i = index[r : r + 8, y : y + 128]
        low.append(i & 127)
        high.append(i >> 7)

    def at_time(t, carry):
        found = [jnp.zeros((8, 128), jnp.float32) for _ in pieces]
        for h in range(traces.shape[1]):
            row = jnp.broadcast_to(traces[t, h : h + 1], (8, 128))
            for p in range(len(pieces)):
                value = jnp.take_along_axis(row, low[p], axis=1, mode="promise_in_bounds")
                found[p] = jnp.where(high[p] == h, value, found[p])
        for (r, y), value in zip(pieces, found):
            for i in range(8):
                inject[t, r + i, :, y : y + 128] = value[i : i + 1]
        return carry

    lax.fori_loop(0, traces.shape[0], at_time, 0)


def wave_kernel(
    count,
    wave_now, wave_prev, coefs_here, inject_here,
    wave_out, snaps,
    even, odd, coefs, inject, send, halo, own, zero,
    local_sem, first_send, first_recv, send_sem, recv_sem, snap_send, snap_recv, snap_local, zero_sem,
):
    width = wave_now.shape[1]
    shot = lax.axis_index("shot")
    me = lax.axis_index("gx")
    has_left = me > 0
    has_right = me < count - 1
    sides = ((0, has_left, me - 1), (1, has_right, me + 1))

    barrier = pltpu.get_barrier_semaphore()
    for _, there, other in sides:
        @pl.when(there)
        def _():
            pl.semaphore_signal(barrier, inc=1, device_id=(shot, other), device_id_type=MESH)

    loads = [
        pltpu.make_async_copy(source, target.at[:, pl.ds(pad, width)], local_sem.at[i])
        for i, (source, target, pad) in enumerate((
            (wave_now, even, DEEP), (wave_prev, odd, DEEP),
            (coefs_here, coefs, 2), (inject_here, inject, 2),
        ))
    ]
    for load in loads:
        load.start()

    def first_copies(side, other, place):
        found = []
        for i, (source, target, pad) in enumerate((
            (wave_prev, odd, DEEP), (coefs_here, coefs, 2), (inject_here, inject, 2),
        )):
            start = pad - 2 if place == 0 else pad + width
            found.append(pltpu.make_async_remote_copy(
                src_ref=source.at[:, pl.ds(side * (width - 2), 2)],
                dst_ref=target.at[:, pl.ds(start, 2)],
                send_sem=first_send.at[i, side],
                recv_sem=first_recv.at[i, place],
                device_id=(shot, other),
                device_id_type=MESH,
            ))
        return found

    for side, there, _ in sides:
        @pl.when(jnp.logical_not(there))
        def _():
            zero[...] = jnp.zeros(zero.shape, zero.dtype)
            for ref in (even, odd):
                ref[:, pl.ds(side * (width + DEEP), DEEP)] = jnp.zeros(
                    (2, DEEP) + ref.shape[2:], ref.dtype)

    def edge_copies():
        found = []
        for side, there, _ in sides:
            for b in range(SNAPS):
                for f in range(2):
                    found.append((there, pltpu.make_async_copy(
                        zero, snaps.at[b, f, pl.ds(side * 2 * width, width)],
                        zero_sem.at[side, b, f])))
        return found

    for there, copy in edge_copies():
        @pl.when(jnp.logical_not(there))
        def _():
            copy.start()

    pl.semaphore_wait(barrier, has_left.astype(jnp.int32) + has_right.astype(jnp.int32))

    def halo_copy(t, side, other):
        return pltpu.make_async_remote_copy(
            src_ref=send.at[t, side],
            dst_ref=halo.at[t, 1 - side],
            send_sem=send_sem.at[t, side],
            recv_sem=recv_sem.at[t, 1 - side],
            device_id=(shot, other),
            device_id_type=MESH,
        )

    def halo_arrival(t, side, other):
        return pltpu.make_async_remote_copy(
            src_ref=send.at[t, side],
            dst_ref=halo.at[t, side],
            send_sem=send_sem.at[t, side],
            recv_sem=recv_sem.at[t, side],
            device_id=(shot, other),
            device_id_type=MESH,
        )

    def snap_copy(b, side, other, place):
        return pltpu.make_async_remote_copy(
            src_ref=own.at[b],
            dst_ref=snaps.at[b, :, pl.ds(place * 2 * width, width)],
            send_sem=snap_send.at[b, side],
            recv_sem=snap_recv.at[b, place],
            device_id=(shot, other),
            device_id_type=MESH,
        )

    def own_copy(b):
        return pltpu.make_async_copy(own.at[b], snaps.at[b, :, pl.ds(width, width)], snap_local.at[b])

    def send_edges(t, ref):
        for side, there, other in sides:
            @pl.when(there)
            def _():
                send[t, side] = ref[:, pl.ds(DEEP + side * (width - DEEP), DEEP)].astype(jnp.bfloat16)
                halo_copy(t, side, other).start()

    depth, cross = wave_now.shape[2:]
    z = lax.broadcasted_iota(jnp.int32, (depth, cross), 0)
    y = lax.broadcasted_iota(jnp.int32, (depth, cross), 1)

    def shift_z(u, move):
        moved = pltpu.roll(u, (-move) % depth, 0)
        inside = (z < depth - move) if move > 0 else (z >= -move)
        return jnp.where(inside, moved, 0.0)

    def shift_y(u, move):
        moved = pltpu.roll(u, (-move) % cross, 1)
        inside = (y < cross - move) if move > 0 else (y >= -move)
        return jnp.where(inside, moved, 0.0)

    def advance(now, prev, t, x):
        centre, cx, cz, cy, cm = (coefs[i, x + 2] for i in range(5))
        row = jnp.broadcast_to(inject[t, x + 2], (depth, cross))
        for f in range(2):
            u = now[f, x + 4]
            before = now[f, x + 3]
            after = now[f, x + 5]
            total = centre * u - prev[f, x + 4]
            total += cx * ((before + after) - (now[f, x + 2] + now[f, x + 6]) * 0.0625)
            far_z = shift_z(u, 2) + shift_z(u, -2)
            total += cz * ((shift_z(u, 1) + shift_z(u, -1)) - far_z * 0.0625)
            far_y = shift_y(u, 2) + shift_y(u, -2)
            total += cy * ((shift_y(u, 1) + shift_y(u, -1)) - far_y * 0.0625)
            across = after - before
            total += cm * (shift_z(across, 1) - shift_z(across, -1))
            if f == 1:
                total += jnp.where(z == 0, row, 0.0)
            prev[f, x + 4] = total

    loads[0].wait()
    send_edges(0, even)
    for side, there, other in sides:
        @pl.when(there)
        def _():
            for copy in first_copies(side, other, 1 - side):
                copy.start()
    for load in loads[1:]:
        load.wait()

    def run(now, prev, t, first, number, unroll):
        def one(i, c):
            advance(now, prev, t, first + i)
            return c

        lax.fori_loop(0, number, one, 0, unroll=unroll)

    def pair(p, carry):
        t = 2 * p

        @pl.when(p % 2 == 0)
        def _():
            b = p // 2
            own[b] = even[:, pl.ds(DEEP, width)].astype(jnp.bfloat16)
            own_copy(b).start()
            for side, there, other in sides:
                @pl.when(there)
                def _():
                    snap_copy(b, side, other, 1 - side).start()

        run(even, odd, t, 2, width - 4, 4)
        run(odd, even, t + 1, 4, width - 8, 4)
        for side, there, other in sides:
            @pl.when(there)
            def _():
                halo_arrival(p, side, other).wait_recv()
                even[:, pl.ds(side * (width + DEEP), DEEP)] = halo[p, side].astype(jnp.float32)

                @pl.when(p == 0)
                def _():
                    for copy in first_copies(side, other, side):
                        copy.wait_recv()

                run(even, odd, t, side * (width + 2) - 2, 2, 2)
        for side, _, _ in sides:
            run(even, odd, t, side * (width - 2), 2, 2)
        for side, _, _ in sides:
            run(odd, even, t + 1, side * (width - 4), 4, 4)

        @pl.when(p < PAIRS - 1)
        def _():
            send_edges(p + 1, even)

        return carry

    lax.fori_loop(0, PAIRS, pair, 0)

    store = pltpu.make_async_copy(even.at[:, pl.ds(DEEP, width)], wave_out, local_sem.at[0])
    store.start()
    for side, there, other in sides:
        @pl.when(there)
        def _():
            def drain(t, c):
                halo_copy(t, side, other).wait_send()
                return c

            lax.fori_loop(0, PAIRS, drain, 0)
            for copy in first_copies(side, other, 1 - side):
                copy.wait_send()
            for b in range(SNAPS):
                snap_copy(b, side, other, 1 - side).wait_send()
                snap_copy(b, side, other, side).wait_recv()
    for there, copy in edge_copies():
        @pl.when(jnp.logical_not(there))
        def _():
            copy.wait()
    for b in range(SNAPS):
        own_copy(b).wait()
    store.wait()


def correlate_kernel(lags, snaps, image):
    group, width = image.shape[:2]

    def one(k, carry):
        h = lags[pl.program_id(0) * group + k] - HALF
        for x in range(width):
            terms = [snaps[b, 0, HALF - h + x] * snaps[b, 1, HALF + h + x] for b in range(SNAPS)]
            image[k, x] = (terms[0] + terms[1]) + (terms[2] + terms[3])
        return carry

    lax.fori_loop(0, group, one, 0)


def body(count, wave_now, wave_prev, courant, epsilon, tilt, trace_index, traces, lag_list):
    _, width, depth, cross = wave_now.shape
    vmem = pl.BlockSpec(memory_space=pltpu.VMEM)
    whole = pl.BlockSpec(memory_space=pl.ANY)
    coefs, inject = pl.pallas_call(
        prep_kernel,
        out_shape=(
            jax.ShapeDtypeStruct((5, width, depth, cross), jnp.float32),
            jax.ShapeDtypeStruct((STEPS, width, 1, cross), jnp.float32),
        ),
        in_specs=[vmem] * 5,
        out_specs=(vmem, vmem),
        compiler_params=pltpu.CompilerParams(vmem_limit_bytes=LIMIT),
    )(courant, epsilon, tilt, trace_index, traces.reshape(STEPS, -1, 128))

    state = pltpu.VMEM((2, width + 2 * DEEP, depth, cross), jnp.float32)
    edges = pltpu.VMEM((PAIRS, 2, 2, DEEP, depth, cross), jnp.bfloat16)
    dma = pltpu.SemaphoreType.DMA
    wave_out, snaps = pl.pallas_call(
        functools.partial(wave_kernel, count),
        out_shape=(
            jax.ShapeDtypeStruct(wave_now.shape, jnp.float32),
            jax.ShapeDtypeStruct((SNAPS, 2, 3 * width, depth, cross), jnp.bfloat16),
        ),
        in_specs=[whole] * 4,
        out_specs=(whole, whole),
        scratch_shapes=[
            state, state,
            pltpu.VMEM((5, width + 4, depth, cross), jnp.float32),
            pltpu.VMEM((STEPS, width + 4, 1, cross), jnp.float32),
            edges, edges,
            pltpu.VMEM((SNAPS, 2, width, depth, cross), jnp.bfloat16),
            pltpu.VMEM((width, depth, cross), jnp.bfloat16),
            dma((4,)),
            dma((3, 2)),
            dma((3, 2)),
            dma((PAIRS, 2)),
            dma((PAIRS, 2)),
            dma((SNAPS, 2)),
            dma((SNAPS, 2)),
            dma((SNAPS,)),
            dma((2, SNAPS, 2)),
        ],
        compiler_params=pltpu.CompilerParams(
            collective_id=0, has_side_effects=True, vmem_limit_bytes=LIMIT
        ),
    )(wave_now, wave_prev, coefs, inject)

    image_out = pl.pallas_call(
        correlate_kernel,
        out_shape=jax.ShapeDtypeStruct((LAGS, width, depth, cross), jnp.bfloat16),
        grid_spec=pltpu.PrefetchScalarGridSpec(
            num_scalar_prefetch=1,
            grid=(LAGS // GROUP,),
            in_specs=[vmem],
            out_specs=pl.BlockSpec((GROUP, width, depth, cross), lambda k, lags: (k, 0, 0, 0)),
        ),
        compiler_params=pltpu.CompilerParams(vmem_limit_bytes=LIMIT),
    )(lag_list, snaps)
    return (image_out, wave_out)


def solution(mesh):
    placed = (
        P("shot", "gx", None, None),
        P("shot", "gx", None, None),
        P("gx", "shot", None),
        P("gx", "shot", None),
        P("gx", "shot", None),
        P("gx", "shot"),
        P("shot", None),
        P(),
    )
    return jax.shard_map(
        functools.partial(body, mesh.shape["gx"]),
        mesh=mesh,
        in_specs=placed,
        out_specs=(P("shot", "gx", None, None), P("shot", "gx", None, None)),
        check_vma=False,
    )
```
